512 devices in a mesh: grp: 8 (over x, core), dom: 64 (over y, z).
Axes of the slice: x: 4, y: 4, z: 16, core: 2. Of those that a mesh axis runs over, the one named last changes fastest.
Arguments:
- nodes: bfloat16 [131072, 512], P(('grp', 'dom')), may hold values from -6 to 6
- w_send: bfloat16 [512, 256], replicated, may hold values from -0.1875 to 0.1875
- w_recv: bfloat16 [512, 256], replicated, may hold values from -0.1875 to 0.1875
- edge_bias: float32 [256], replicated, may hold values from -4 to 4
- w_msg: bfloat16 [256, 512], replicated, may hold values from -0.375 to 0.375
- msg_gain: float32 [512], replicated, may hold values from 0.5 to 1.5
- w_self: bfloat16 [512, 512], replicated, may hold values from -0.1875 to 0.1875
- w_agg: bfloat16 [512, 512], replicated, may hold values from -0.09375 to 0.09375
- w_coarse_in: bfloat16 [512, 256], replicated, may hold values from -0.25 to 0.25
- coarse_bias: float32 [256], replicated, may hold values from -4 to 4
- w_coarse_out: bfloat16 [256, 512], replicated, may hold values from -0.375 to 0.375
- halo_send: int32 [512, 2, 128], P(('grp', 'dom')), may hold values from 0 to 255
- neighbours: int32 [131072, 8], P(('grp', 'dom')), may hold values from 0 to 511
- edge_mask: int32 [131072, 8], P(('grp', 'dom')), may hold values 0 or 1
- restrict_ids: int32 [131072], P(('grp', 'dom')), may hold values from 0 to 31
- coarse_holder_index: int32 [32768, 1], P(('grp', 'dom')), may hold values from 0 to 63; in each aligned block of 64 rows (0 to 63, 64 to 127, ...) at most 2 rows name the same one
- coarse_slot: int32 [32768, 1], P(('grp', 'dom')), may hold values from 0 to 15
Outputs:
- updated: bfloat16 [131072, 512], P(('grp', 'dom'))
The draws below stay inside these ranges and needn't reach their ends.
Inputs may be any that keep to these rules, and one draw needn't show every extreme that they name: `coarse_holder_index`: among the restricted rows of one partition no owner is named more than 2 times, and in every draw some owner is named exactly 2 times.
All inputs are finite; a program needn't handle non-finite values. No bound on the sum of `edge_mask` on one device may be relied on, other than what follows from the above.
Results may differ from the reference program's by a relative error of at most 0.0053.
Values may be sent and summed in bfloat16 or wider, within the bound.
A program may use at most 64 MiB of HBM per device.

```python
import math
import jax
import jax.numpy as jnp
import numpy as np
from jax import lax

D = 512
EH = 256
NODE_DEV = 256
HROWS = 128
DEG = 8
RBLOCK = 128
RCOARSE = 32
RROWS = 64
CAP = 2
CSLOT = 16
DEVICES_NODES = 131072
N_GRP = 8
N_DOM = 64
DEVICES = 512


def plant(entries, rng, low, largest):
    longest = entries.shape.index(max(entries.shape))
    spots = []
    for shift in (0, 1):
        where = [jax.random.randint(jax.random.fold_in(rng, axis), (), 0, length) for axis, length in enumerate(entries.shape)]
        where[longest] = (where[longest] + shift) % entries.shape[longest]
        spots.append(tuple(where))
    return entries.at[spots[0]].set(low).at[spots[1]].set(largest)


def shard_levels(key, extent, shards, smallest, top_value):
    level = 1.0
    for axis_at, blocks in shards:
        draws = jax.random.uniform(jax.random.fold_in(jax.random.fold_in(key, 6), axis_at), (blocks,), jnp.float32, smallest / len(shards), top_value / len(shards))
        level = level * jnp.repeat(jnp.exp(draws), extent[axis_at] // blocks).reshape((-1,) + (1,) * (len(extent) - 1 - axis_at))
    return level


def assign_block(rng, own, number, rows, count, top, limit, slope):
    ranking = jax.random.permutation(rng, count)
    packed, usual = shares(count, rows * top, limit, slope, True), shares(count, rows * top, limit, slope, False)
    places = jnp.arange(count)

    def named(sizes, offset_by):
        used = int((sizes > 0).sum())
        fixed = max(1, used // 4)
        shifted = fixed + (places - fixed + offset_by * (used - fixed)) % max(1, count - fixed)
        return jnp.zeros((count,), jnp.int32).at[ranking[jnp.where(places < fixed, places, shifted)]].set(jnp.asarray(sizes, jnp.int32))

    sizes = jnp.where(number % 4 == 0, named(packed, number // 4), named(usual, number - number // 4 - 1))
    mixed = jax.random.permutation(jax.random.fold_in(own, 3), count)
    donor, taker = mixed[0:count // 2 * 2:2], mixed[1:count // 2 * 2:2]
    slack = jnp.minimum(sizes[donor] - 1, limit - sizes[taker]) // 2
    slack = jnp.where((donor == ranking[0]) | (taker == ranking[0]) | (sizes[taker] == 0), 0, jnp.maximum(slack, 0))
    shifted = jax.random.randint(jax.random.fold_in(own, 4), (count // 2,), 0, 1 << 20) % (slack + 1)
    sizes = sizes.at[donor].add(-shifted).at[taker].add(shifted)
    items = jnp.searchsorted(jnp.cumsum(sizes), jnp.arange(rows * top), side="right").astype(jnp.int32)
    listing = items.reshape(top, rows).T
    listing = listing[jax.random.permutation(jax.random.fold_in(own, 1), rows)]
    offset_by = jax.random.randint(jax.random.fold_in(own, 2), (rows, 1), 0, top)
    return jnp.take_along_axis(listing, (jnp.arange(top)[None, :] + offset_by) % top, axis=1)


def shares(count, total, most, lean, full):
    loads = [(1 << 20) // math.isqrt(grade ** lean) + 1 for grade in range(1, count + 1)]
    largest = most if full else min(most, max(-(-total // count), total * loads[0] // sum(loads)))
    least = 1 if total - largest >= count - 1 else 0
    counts, rest = [largest] + [least] * (count - 1), total - largest - least * (count - 1)
    while rest > 0:
        candidates = [i for i in range(1, count) if counts[i] < largest] or [i for i in range(1, count) if counts[i] < most]
        pool, remaining = sum([loads[i] for i in candidates]), rest
        for i in candidates:
            addition = min(most - counts[i], max(1, remaining * loads[i] // pool), rest)
            counts[i] = counts[i] + addition
            rest = rest - addition
    return np.array(counts)


def bell_draw(stream_key, shape, spread, bound, cuts=(), kind=jnp.bfloat16):
    factor_of = shard_levels(stream_key, shape, cuts, -0.22, 0.18) if cuts else 1.0
    values = jax.random.normal(stream_key, shape, jnp.float32) * spread * factor_of
    return jnp.minimum(jnp.maximum(values, -bound), bound).astype(kind)


def setup_inputs(seed: int = 0) -> dict:
    seeds = jax.random.split(jax.random.key(seed), 18)
    nodes = bell_draw(seeds[0], (DEVICES_NODES, D), 1.0, 6.0, ((0, 512),))
    w_send = bell_draw(seeds[1], (D, EH), (2 * D) ** -0.5, 0.1875)
    w_recv = bell_draw(seeds[2], (D, EH), (2 * D) ** -0.5, 0.1875)
    edge_bias = bell_draw(seeds[3], (EH,), 1.0, 4.0, (), jnp.float32)
    w_msg = bell_draw(seeds[4], (EH, D), EH ** -0.5, 0.375)
    msg_gain = jnp.clip(1.0 + 0.1 * jax.random.normal(seeds[5], (D,), jnp.float32), 0.5, 1.5)
    w_self = bell_draw(seeds[6], (D, D), (2 * D) ** -0.5, 0.1875)
    w_agg = bell_draw(seeds[7], (D, D), (8 * D) ** -0.5, 0.09375)
    w_coarse_in = bell_draw(seeds[8], (D, EH), D ** -0.5, 0.25)
    coarse_bias = bell_draw(seeds[9], (EH,), 1.0, 4.0, (), jnp.float32)
    w_coarse_out = bell_draw(seeds[10], (EH, D), EH ** -0.5, 0.375)
    halo_send = plant(jax.random.randint(seeds[11], (DEVICES, 2, HROWS), 0, NODE_DEV), jax.random.fold_in(seeds[11], 1), 0, NODE_DEV - 1).astype(jnp.int32)
    neighbours = plant(jax.random.randint(seeds[12], (DEVICES_NODES, DEG), 0, NODE_DEV + 2 * HROWS), jax.random.fold_in(seeds[12], 1), 0, (NODE_DEV + 2 * HROWS) - 1).astype(jnp.int32)
    edge_mask = plant((jax.random.randint(seeds[13], (DEVICES_NODES, DEG), 0, 8) < 7).astype(jnp.int32), jax.random.fold_in(seeds[13], 1), 0, 1)
    restrict_ids = plant(jax.random.randint(seeds[14], (DEVICES_NODES,), 0, RCOARSE), jax.random.fold_in(seeds[14], 1), 0, RCOARSE - 1).astype(jnp.int32)
    coarse_holder_index_keys = jax.random.split(jax.random.fold_in(seeds[15], 1), (DEVICES * RROWS) // RROWS)
    coarse_holder_index_turns = jax.random.permutation(jax.random.fold_in(seeds[15], 3), (DEVICES * RROWS) // RROWS)
    coarse_holder_index = jax.vmap(lambda own, number: assign_block(jax.random.fold_in(seeds[15], 2), own, number, RROWS, N_DOM, 1, CAP, 2))(coarse_holder_index_keys, coarse_holder_index_turns).reshape((DEVICES * RROWS, 1))
    coarse_slot = plant(jax.random.randint(seeds[16], (DEVICES * RROWS, 1), 0, CSLOT), jax.random.fold_in(seeds[16], 1), 0, CSLOT - 1).astype(jnp.int32)
    return {"nodes": nodes, "w_send": w_send, "w_recv": w_recv, "edge_bias": edge_bias, "w_msg": w_msg, "msg_gain": msg_gain, "w_self": w_self, "w_agg": w_agg, "w_coarse_in": w_coarse_in, "coarse_bias": coarse_bias, "w_coarse_out": w_coarse_out, "halo_send": halo_send, "neighbours": neighbours, "edge_mask": edge_mask, "restrict_ids": restrict_ids, "coarse_holder_index": coarse_holder_index, "coarse_slot": coarse_slot}


def restrict_dev(args):
    x_dev, ids = args
    blocks = NODE_DEV // RBLOCK
    member = (ids.reshape(blocks, RBLOCK)[:, :, None] == jnp.arange(RCOARSE, dtype=jnp.int32)[None, None, :]).astype(jnp.float32)
    summed = jnp.einsum('bic,bid->bcd', member, x_dev.reshape(blocks, RBLOCK, D).astype(jnp.float32))
    return (summed * 0.25).astype(jnp.bfloat16).reshape(RROWS, D)

def reference(nodes, w_send, w_recv, edge_bias, w_msg, msg_gain, w_self, w_agg, w_coarse_in, coarse_bias, w_coarse_out, halo_send, neighbours, edge_mask, restrict_ids, coarse_holder_index, coarse_slot):
    parts = N_GRP * N_DOM
    proj = jnp.dot(nodes, w_send, preferred_element_type=jnp.float32).astype(jnp.bfloat16).reshape(N_GRP, N_DOM, NODE_DEV, EH)
    sends = halo_send.reshape(N_GRP, N_DOM, 2, HROWS)
    picked = jax.vmap(jax.vmap(lambda table_rows, which: table_rows[which]))(proj, sends)
    from_lower = jnp.roll(picked[:, :, 1], 1, axis=0)
    upper_level_input = jnp.roll(picked[:, :, 0], -1, axis=0)
    tables = jnp.concatenate([proj, from_lower, upper_level_input], axis=2).reshape(parts, NODE_DEV + 2 * HROWS, EH)
    x_parts = nodes.reshape(parts, NODE_DEV, D)
    ids_parts = restrict_ids.reshape(parts, NODE_DEV)
    restricted = lax.map(restrict_dev, (x_parts, ids_parts))
    coarse_in = jnp.dot(restricted.reshape(-1, D), w_coarse_in, preferred_element_type=jnp.float32).astype(jnp.bfloat16)
    group_of = (jnp.arange(parts * RROWS, dtype=jnp.int32) // (N_DOM * RROWS)).astype(jnp.int32)
    segment = group_of * (N_DOM * CSLOT) + coarse_holder_index[:, 0] * CSLOT + coarse_slot[:, 0]
    summed = jax.ops.segment_sum(coarse_in.astype(jnp.float32), segment, num_segments=N_GRP * N_DOM * CSLOT)
    coarse_hid = jax.nn.silu(summed + coarse_bias).astype(jnp.bfloat16)
    coarse_out = jnp.dot(coarse_hid, w_coarse_out, preferred_element_type=jnp.float32).astype(jnp.bfloat16)
    corr_rows = coarse_out[segment].reshape(parts, RROWS, D)

    def one_part(args):
        x_dev, table, nbr, mask, ids, corr = args
        recv_part = jnp.dot(x_dev, w_recv, preferred_element_type=jnp.float32)
        agg = jnp.zeros((NODE_DEV, D), jnp.float32)
        for slot in range(DEG):
            pre = table[nbr[:, slot]].astype(jnp.float32) + recv_part + edge_bias
            hid = jax.nn.silu(pre).astype(jnp.bfloat16)
            msg = jnp.dot(hid, w_msg, preferred_element_type=jnp.float32)
            mean = lax.optimization_barrier(jnp.mean(msg, axis=1, keepdims=True))
            var = lax.optimization_barrier(jnp.mean((msg - mean) ** 2, axis=1, keepdims=True))
            normed = (msg - mean) / jnp.sqrt(var + 1e-05) * msg_gain
            agg = agg + normed * mask[:, slot:slot + 1].astype(jnp.float32)
        agg = agg.astype(jnp.bfloat16)
        change = jax.nn.silu(jnp.dot(x_dev, w_self, preferred_element_type=jnp.float32) + jnp.dot(agg, w_agg, preferred_element_type=jnp.float32))
        blocks = NODE_DEV // RBLOCK
        member = (ids.reshape(blocks, RBLOCK)[:, :, None] == jnp.arange(RCOARSE, dtype=jnp.int32)[None, None, :]).astype(jnp.float32)
        corr_nodes = jnp.einsum('bic,bcd->bid', member, corr.reshape(blocks, RCOARSE, D).astype(jnp.float32)).reshape(NODE_DEV, D)
        return (x_dev.astype(jnp.float32) + change + corr_nodes).astype(jnp.bfloat16)
    result = lax.map(one_part, (x_parts, tables, neighbours.reshape(parts, NODE_DEV, DEG), edge_mask.reshape(parts, NODE_DEV, DEG), ids_parts, corr_rows))
    return result.reshape(parts * NODE_DEV, D)
```

```python
import jax
import jax.numpy as jnp
from jax import lax
from jax.experimental import pallas as pl
from jax.experimental.pallas import tpu as pltpu
from jax.sharding import PartitionSpec as P

MESH = pl.DeviceIdType.MESH
BF = jnp.bfloat16
F32 = jnp.float32
I32 = jnp.int32

GRP = 8
DOM = 64
ZS = 16
YS = 4
N = 256
D = 512
EH = 256
H = 128
DEG = 8
ROWS = 64
RC = 32
RB = 128
SLOTS = 16
MSG = EH + 128


def iota(shape, dim):
    return lax.broadcasted_iota(I32, shape, dim)


def dot(a, b):
    return jnp.dot(a, b, preferred_element_type=F32)


def silu(v):
    return v * (0.5 + 0.5 * jnp.tanh(0.5 * v))


def kernel(
    nodes_h,
    w_send_h,
    w_recv_h,
    w_msg_h,
    w_self_h,
    w_agg_h,
    w_cin_h,
    w_cout_h,
    edge_bias,
    gain,
    coarse_bias,
    halo_ids,
    nbr,
    mask,
    ids,
    own,
    slot,
    out,
    nodes,
    w_send,
    w_recv,
    w_msg,
    w_self,
    w_agg,
    w_cin,
    w_cout,
    table,
    halo_out,
    send_buf,
    recv_buf,
    back_buf,
    ret_buf,
    agg,
    base,
    load_sem,
    halo_ssem,
    halo_rsem,
    c_ssem,
    c_rsem,
    r_ssem,
    r_rsem,
    own_sem,
):
    g = lax.axis_index("grp")
    me = lax.axis_index("dom")
    lower = lax.rem(g + GRP - 1, GRP)
    upper = lax.rem(g + 1, GRP)

    loads = {}
    for i, (name, src, dst) in enumerate(
        (
            ("nodes", nodes_h, nodes),
            ("w_cin", w_cin_h, w_cin),
            ("w_send", w_send_h, w_send),
            ("w_recv", w_recv_h, w_recv),
            ("w_msg", w_msg_h, w_msg),
            ("w_self", w_self_h, w_self),
            ("w_agg", w_agg_h, w_agg),
            ("w_cout", w_cout_h, w_cout),
        )
    ):
        loads[name] = pltpu.make_async_copy(src, dst, load_sem.at[i])
        loads[name].start()

    barrier = pltpu.get_barrier_semaphore()

    def greet(k, carry):
        pl.semaphore_signal(
            barrier, inc=1, device_id=(g, lax.rem(me + k, DOM)), device_id_type=MESH
        )
        return carry

    lax.fori_loop(1, DOM, greet, 0)
    for t in (lower, upper):
        pl.semaphore_signal(barrier, inc=1, device_id=(t, me), device_id_type=MESH)

    own_row = own[...].astype(F32)
    eye = iota((ROWS, ROWS), 0) == iota((ROWS, ROWS), 1)
    own_col = jnp.sum(jnp.where(eye, own_row, 0.0), axis=1, keepdims=True)
    before = (own_col == own_row) & (iota((ROWS, ROWS), 0) < iota((ROWS, ROWS), 1))
    rank = jnp.sum(before.astype(F32), axis=0, keepdims=True)
    pos = (own_row * 2.0 + rank).astype(I32)
    placed = iota((2 * DOM, ROWS), 0) == pos
    place = placed.astype(F32).astype(BF)
    slot_col = (
        jnp.sum(jnp.where(placed, slot[...].astype(F32) + 1.0, 0.0), axis=1, keepdims=True) - 1.0
    )
    row_of = ids[...] + (iota((1, N), 1) // RB) * RC
    member = (iota((ROWS, N), 0) == row_of).astype(F32).astype(BF)
    spread = dot(place, member).T.astype(BF)

    loads["nodes"].wait()
    restricted = (dot(member, nodes[...]) * 0.25).astype(BF)
    loads["w_cin"].wait()
    coarse_in = dot(restricted, w_cin[...]).astype(BF)
    outgoing = dot(place, coarse_in).astype(BF)
    send_buf[:, :, 0:EH] = outgoing.reshape(DOM, 2, EH)
    send_buf[:, :, EH:MSG] = (
        jnp.broadcast_to(slot_col, (2 * DOM, 128)).astype(BF).reshape(DOM, 2, 128)
    )

    loads["w_send"].wait()
    proj = dot(nodes[...], w_send[...]).T.astype(BF)
    table[:, 0:N] = proj
    for i in range(2):
        pick = (iota((N, H), 0) == halo_ids[0, i : i + 1, :]).astype(F32).astype(BF)
        halo_out[i] = dot(proj, pick).astype(BF)

    pl.semaphore_wait(barrier, DOM - 1 + 2)

    mine = pltpu.make_async_copy(send_buf.at[me], recv_buf.at[me], own_sem.at[0])
    mine.start()

    def send_rows(k, carry):
        t = lax.rem(me + k, DOM)
        pltpu.make_async_remote_copy(
            src_ref=send_buf.at[t],
            dst_ref=recv_buf.at[me],
            send_sem=c_ssem,
            recv_sem=c_rsem,
            device_id=(g, t),
            device_id_type=MESH,
        ).start()
        return carry

    lax.fori_loop(1, DOM, send_rows, 0)

    halos = []
    for i, t in ((0, lower), (1, upper)):
        c = pltpu.make_async_remote_copy(
            src_ref=halo_out.at[i],
            dst_ref=table.at[:, pl.ds(N + H * (1 - i), H)],
            send_sem=halo_ssem.at[i],
            recv_sem=halo_rsem.at[i],
            device_id=(t, me),
            device_id_type=MESH,
        )
        c.start()
        halos.append(c)

    loads["w_recv"].wait()
    recv = (dot(nodes[...], w_recv[...]) + edge_bias[...]).T
    loads["w_self"].wait()
    base[...] = dot(nodes[...], w_self[...])
    loads["w_msg"].wait()
    w_msg_t = w_msg[...].T
    agg[...] = jnp.zeros_like(agg)
    for c in halos:
        c.wait()

    def edges(k):
        pick = (iota((N + 2 * H, N), 0) == nbr[k : k + 1, :]).astype(F32).astype(BF)
        hid = silu(dot(table[...], pick) + recv).astype(BF)
        msg = dot(w_msg_t, hid)
        mean = jnp.mean(msg, axis=0, keepdims=True)
        msg = msg - mean
        var = jnp.mean(msg * msg, axis=0, keepdims=True)
        scale = lax.rsqrt(var + 1e-05) * mask[k : k + 1, :].astype(F32)
        agg[...] += msg * scale

    for k in range(DEG // 2):
        edges(k)

    mine.wait()
    pltpu.make_async_copy(
        recv_buf.at[pl.ds(0, DOM - 1)], recv_buf.at[pl.ds(0, DOM - 1)], c_rsem
    ).wait()
    got = recv_buf[...].reshape(2 * DOM, MSG)
    holds = (
        (iota((2 * DOM, SLOTS), 1).astype(F32) == got[:, EH : EH + 1].astype(F32))
        .astype(F32)
        .astype(BF)
    )
    summed = lax.dot_general(
        holds, got[:, 0:EH], (((0,), (0,)), ((), ())), preferred_element_type=F32
    )
    coarse_hid = silu(summed + coarse_bias[...]).astype(BF)
    back_buf[...] = dot(holds, coarse_hid).astype(BF).reshape(DOM, 2, EH)
    mine2 = pltpu.make_async_copy(back_buf.at[me], ret_buf.at[me], own_sem.at[1])
    mine2.start()

    def send_back(k, carry):
        t = lax.rem(me + k, DOM)
        pltpu.make_async_remote_copy(
            src_ref=back_buf.at[t],
            dst_ref=ret_buf.at[me],
            send_sem=r_ssem,
            recv_sem=r_rsem,
            device_id=(g, t),
            device_id_type=MESH,
        ).start()
        return carry

    lax.fori_loop(1, DOM, send_back, 0)

    for k in range(DEG // 2, DEG):
        edges(k)
    loads["w_agg"].wait()
    aggregate = (agg[...].T * gain[...]).astype(BF)
    change = silu(base[...] + dot(aggregate, w_agg[...]))
    base[...] = nodes[...].astype(F32) + change
    loads["w_cout"].wait()

    mine2.wait()
    pltpu.make_async_copy(
        ret_buf.at[pl.ds(0, DOM - 1)], ret_buf.at[pl.ds(0, DOM - 1)], r_rsem
    ).wait()
    coarse_out = dot(ret_buf[...].reshape(2 * DOM, EH), w_cout[...]).astype(BF)
    out[...] = (base[...] + dot(spread, coarse_out)).astype(BF)

    pltpu.make_async_copy(
        send_buf.at[pl.ds(0, DOM - 1)], send_buf.at[pl.ds(0, DOM - 1)], c_ssem
    ).wait()
    pltpu.make_async_copy(
        back_buf.at[pl.ds(0, DOM - 1)], back_buf.at[pl.ds(0, DOM - 1)], r_ssem
    ).wait()


def local(
    nodes,
    w_send,
    w_recv,
    edge_bias,
    w_msg,
    msg_gain,
    w_self,
    w_agg,
    w_coarse_in,
    coarse_bias,
    w_coarse_out,
    halo_send,
    neighbours,
    edge_mask,
    restrict_ids,
    coarse_holder_index,
    coarse_slot,
):
    hbm = pl.BlockSpec(memory_space=pltpu.HBM)
    vmem = pl.BlockSpec(memory_space=pltpu.VMEM)
    dma = pltpu.SemaphoreType.DMA
    return pl.pallas_call(
        kernel,
        out_shape=jax.ShapeDtypeStruct((N, D), BF),
        in_specs=[hbm] * 8 + [vmem] * 9,
        out_specs=vmem,
        scratch_shapes=[
            pltpu.VMEM((N, D), BF),
            pltpu.VMEM((D, EH), BF),
            pltpu.VMEM((D, EH), BF),
            pltpu.VMEM((EH, D), BF),
            pltpu.VMEM((D, D), BF),
            pltpu.VMEM((D, D), BF),
            pltpu.VMEM((D, EH), BF),
            pltpu.VMEM((EH, D), BF),
            pltpu.VMEM((EH, N + 2 * H), BF),
            pltpu.VMEM((2, EH, H), BF),
            pltpu.VMEM((DOM, 2, MSG), BF),
            pltpu.VMEM((DOM, 2, MSG), BF),
            pltpu.VMEM((DOM, 2, EH), BF),
            pltpu.VMEM((DOM, 2, EH), BF),
            pltpu.VMEM((D, N), F32),
            pltpu.VMEM((N, D), F32),
            dma((8,)),
            dma((2,)),
            dma((2,)),
            dma(()),
            dma(()),
            dma(()),
            dma(()),
            dma((2,)),
        ],
        compiler_params=pltpu.CompilerParams(
            collective_id=0, has_side_effects=True, vmem_limit_bytes=60 * 1024 * 1024
        ),
    )(
        nodes,
        w_send,
        w_recv,
        w_msg,
        w_self,
        w_agg,
        w_coarse_in,
        w_coarse_out,
        edge_bias.reshape(1, EH),
        msg_gain.reshape(1, D),
        coarse_bias.reshape(1, EH),
        halo_send,
        neighbours.T,
        edge_mask.T,
        restrict_ids.reshape(1, N),
        coarse_holder_index.T,
        coarse_slot.T,
    )


def solution(mesh):
    part = P(("grp", "dom"))
    return jax.shard_map(
        local,
        mesh=mesh,
        in_specs=(part,) + (P(),) * 10 + (part,) * 6,
        out_specs=part,
        check_vma=False,
    )
```

```python
import jax
import jax.numpy as jnp
from jax import lax
from jax.experimental import pallas as pl
from jax.experimental.pallas import tpu as pltpu
from jax.sharding import PartitionSpec as P

MESH = pl.DeviceIdType.MESH
BF = jnp.bfloat16
F32 = jnp.float32
I32 = jnp.int32

GRP = 8
DOM = 64
ZS = 16
YS = 4
N = 256
D = 512
EH = 256
H = 128
DEG = 8
ROWS = 64
RC = 32
RB = 128
SLOTS = 16
PZ = 4
PROC = YS * PZ
OWN = DOM // PROC
CAP = 2 * OWN
NODES_C = OWN * SLOTS


def iota(shape, dim):
    return lax.broadcasted_iota(I32, shape, dim)


def dot(a, b):
    return jnp.dot(a, b, preferred_element_type=F32)


def silu(v):
    return v * (0.5 + 0.5 * jnp.tanh(0.5 * v))


def kernel(*refs):
    ins, (out,), scratch = refs[:17], refs[17:18], refs[18:]
    bufs, rest = scratch[:17], scratch[17:]
    (
        nodes,
        w_cin,
        own,
        slot,
        ids,
        w_send,
        halo_ids,
        w_recv,
        edge_bias,
        w_msg,
        nbr,
        mask,
        w_self,
        gain,
        w_agg,
        coarse_bias,
        w_cout,
    ) = bufs
    (
        table,
        halo_out,
        send_ids,
        recv_ids,
        send_buf,
        recv_buf,
        back_buf,
        ret_buf,
        agg,
        base,
        load_sem,
        halo_ssem,
        halo_rsem,
        i_ssem,
        i_rsem,
        c_ssem,
        c_rsem,
        r_ssem,
        r_rsem,
        own_sem,
    ) = rest
    g = lax.axis_index("grp")
    me = lax.axis_index("dom")
    my_y, my_z = me // ZS, lax.rem(me, ZS)
    lower = lax.rem(g + GRP - 1, GRP)
    upper = lax.rem(g + 1, GRP)
    is_proc = my_z < PZ
    my_proc = jnp.where(is_proc, my_z * YS + my_y, 0)

    def proc_device(j):
        return lax.rem(j, YS) * ZS + j // YS

    loads = [pltpu.make_async_copy(ins[i], bufs[i], load_sem.at[i]) for i in range(17)]
    for i in (2, 3, 4, 0, 1):
        loads[i].start()

    barrier = pltpu.get_barrier_semaphore()
    for t in (lower, upper):
        pl.semaphore_signal(barrier, inc=1, device_id=(t, me), device_id_type=MESH)

    def by_z(k):
        return lax.rem(my_y + k, YS) * ZS + k // YS

    @pl.when(is_proc)
    def _():
        def greet(k, carry):
            t = by_z(k)

            @pl.when(t != me)
            def _():
                pl.semaphore_signal(barrier, inc=1, device_id=(g, t), device_id_type=MESH)

            return carry

        lax.fori_loop(0, DOM, greet, 0)

    for i in range(5, 17):
        loads[i].start()

    for i in (2, 3, 4):
        loads[i].wait()
    own_row = own[...].astype(F32)
    eye = iota((ROWS, ROWS), 0) == iota((ROWS, ROWS), 1)
    own_col = jnp.sum(jnp.where(eye, own_row, 0.0), axis=1, keepdims=True)
    before = (own_col == own_row) & (iota((ROWS, ROWS), 0) < iota((ROWS, ROWS), 1))
    rank = jnp.sum(before.astype(F32), axis=0, keepdims=True).astype(I32)
    pos = own[...] * 2 + rank
    place = (iota((2 * DOM, ROWS), 0) == pos).astype(F32).astype(BF)
    value = (lax.rem(own[...], OWN) * SLOTS + slot[...] + 1).astype(F32)
    at_proc = (iota((PROC, ROWS), 0) == pos // CAP).astype(F32).astype(BF)
    at_lane = jnp.where(iota((128, ROWS), 0) == lax.rem(pos, CAP), value, 0.0).astype(BF)
    coarse_ids = (
        lax.dot_general(at_proc, at_lane, (((1,), (1,)), ((), ())), preferred_element_type=F32)
        - 1.0
    )
    send_ids[...] = coarse_ids.reshape(PROC, 1, 128)
    row_of = ids[...] + (iota((1, N), 1) // RB) * RC
    member = (iota((ROWS, N), 0) == row_of).astype(F32).astype(BF)
    spread = dot(place, member)
    collect = spread.astype(BF)

    pl.semaphore_wait(barrier, jnp.where(is_proc, PROC - 1, PROC) + 2)

    def to_procs(src, dst, ssem, rsem):
        def body(k, carry):
            j = lax.rem(my_z * YS + my_y + k, PROC)
            t = proc_device(j)

            @pl.when(t != me)
            def _():
                pltpu.make_async_remote_copy(
                    src_ref=src.at[j],
                    dst_ref=dst.at[me],
                    send_sem=ssem,
                    recv_sem=rsem,
                    device_id=(g, t),
                    device_id_type=MESH,
                ).start()

            return carry

        lax.fori_loop(0, PROC, body, 0)

    def await_bytes(ref, count, sem):
        part = ref.at[pl.ds(0, count)]
        pltpu.make_async_copy(part, part, sem).wait()

    to_procs(send_ids, recv_ids, i_ssem, i_rsem)
    loads[0].wait()
    restricted = (dot(collect, nodes[...]) * 0.25).astype(BF)
    loads[1].wait()
    coarse_in = dot(restricted, w_cin[...]).astype(BF)
    send_buf[...] = coarse_in.reshape(PROC, CAP, EH)
    to_procs(send_buf, recv_buf, c_ssem, c_rsem)

    loads[5].wait()
    loads[6].wait()
    proj = dot(nodes[...], w_send[...]).T.astype(BF)
    table[:, 0:N] = proj
    halos = []
    for i, t in ((0, lower), (1, upper)):
        pick = (iota((N, H), 0) == halo_ids[0, i : i + 1, :]).astype(F32).astype(BF)
        halo_out[i] = dot(proj, pick).astype(BF)
        c = pltpu.make_async_remote_copy(
            src_ref=halo_out.at[i],
            dst_ref=table.at[:, pl.ds(N + H * (1 - i), H)],
            send_sem=halo_ssem.at[i],
            recv_sem=halo_rsem.at[i],
            device_id=(t, me),
            device_id_type=MESH,
        )
        c.start()
        halos.append(c)

    loads[7].wait()
    loads[8].wait()
    recv = (dot(nodes[...], w_recv[...]) + edge_bias[...]).T
    for i in (9, 10, 11, 12, 13, 14, 15, 16):
        loads[i].wait()
    base[...] = dot(nodes[...], w_self[...])
    w_msg_t = w_msg[...].T
    agg[...] = jnp.zeros_like(agg)
    spread = spread.T.astype(BF)
    for c in halos:
        c.wait()

    for k in range(DEG):
        pick = (iota((N + 2 * H, N), 0) == nbr[k : k + 1, :]).astype(F32).astype(BF)
        hid = silu(dot(table[...], pick) + recv).astype(BF)
        msg = dot(w_msg_t, hid)
        mean = jnp.mean(msg, axis=0, keepdims=True)
        msg = msg - mean
        var = jnp.mean(msg * msg, axis=0, keepdims=True)
        scale = lax.rsqrt(var + 1e-05) * mask[k : k + 1, :].astype(F32)
        agg[...] += msg * scale
    aggregate = (agg[...].T * gain[...]).astype(BF)
    change = silu(base[...] + dot(aggregate, w_agg[...]))
    base[...] = nodes[...].astype(F32) + change

    @pl.when(is_proc)
    def _():
        own_ids = pltpu.make_async_copy(send_ids.at[my_proc], recv_ids.at[me], own_sem.at[0])
        own_rows = pltpu.make_async_copy(send_buf.at[my_proc], recv_buf.at[me], own_sem.at[1])
        own_ids.start()
        own_rows.start()
        own_ids.wait()
        await_bytes(recv_ids, DOM - 1, i_rsem)
        got_ids = recv_ids[...].reshape(DOM, 128).astype(BF)
        total = DOM * CAP
        from_dev = (iota((DOM, total), 0) == iota((DOM, total), 1) // CAP).astype(F32).astype(BF)
        by_lane = lax.dot_general(
            got_ids, from_dev, (((0,), (0,)), ((), ())), preferred_element_type=F32
        )[0:CAP]
        mine = iota((CAP, total), 0) == lax.rem(iota((CAP, total), 1), CAP)
        id_row = jnp.sum(jnp.where(mine, by_lane, 0.0), axis=0, keepdims=True)
        holds = (iota((NODES_C, total), 0).astype(F32) == id_row).astype(F32)
        holds_t = holds.T.astype(BF)
        holds = holds.astype(BF)
        own_rows.wait()
        await_bytes(recv_buf, DOM - 1, c_rsem)
        summed = dot(holds, recv_buf[...].reshape(total, EH))
        coarse_hid = silu(summed + coarse_bias[...]).astype(BF)
        back_buf[...] = dot(holds_t, coarse_hid).astype(BF).reshape(DOM, CAP, EH)

        def send_back(k, carry):
            t = by_z(k)

            @pl.when(t != me)
            def _():
                pltpu.make_async_remote_copy(
                    src_ref=back_buf.at[t],
                    dst_ref=ret_buf.at[my_proc],
                    send_sem=r_ssem,
                    recv_sem=r_rsem,
                    device_id=(g, t),
                    device_id_type=MESH,
                ).start()

            return carry

        lax.fori_loop(0, DOM, send_back, 0)
        own_back = pltpu.make_async_copy(back_buf.at[me], ret_buf.at[my_proc], own_sem.at[2])
        own_back.start()
        own_back.wait()
        await_bytes(send_ids, PROC - 1, i_ssem)
        await_bytes(send_buf, PROC - 1, c_ssem)
        await_bytes(ret_buf, PROC - 1, r_rsem)

    @pl.when(jnp.logical_not(is_proc))
    def _():
        await_bytes(send_ids, PROC, i_ssem)
        await_bytes(send_buf, PROC, c_ssem)
        await_bytes(ret_buf, PROC, r_rsem)

    coarse_out = dot(ret_buf[...].reshape(2 * DOM, EH), w_cout[...]).astype(BF)
    out[...] = (base[...] + dot(spread, coarse_out)).astype(BF)

    @pl.when(is_proc)
    def _():
        await_bytes(back_buf, DOM - 1, r_ssem)


def local(
    nodes,
    w_send,
    w_recv,
    edge_bias,
    w_msg,
    msg_gain,
    w_self,
    w_agg,
    w_coarse_in,
    coarse_bias,
    w_coarse_out,
    halo_send,
    neighbours,
    edge_mask,
    restrict_ids,
    coarse_holder_index,
    coarse_slot,
):
    hbm = pl.BlockSpec(memory_space=pltpu.HBM)
    dma = pltpu.SemaphoreType.DMA
    args = (
        nodes,
        w_coarse_in,
        coarse_holder_index.T,
        coarse_slot.T,
        restrict_ids.reshape(1, N),
        w_send,
        halo_send,
        w_recv,
        edge_bias.reshape(1, EH),
        w_msg,
        neighbours.T,
        edge_mask.T,
        w_self,
        msg_gain.reshape(1, D),
        w_agg,
        coarse_bias.reshape(1, EH),
        w_coarse_out,
    )
    return pl.pallas_call(
        kernel,
        out_shape=jax.ShapeDtypeStruct((N, D), BF),
        in_specs=[hbm] * len(args),
        out_specs=pl.BlockSpec(memory_space=pltpu.VMEM),
        scratch_shapes=[pltpu.VMEM(a.shape, a.dtype) for a in args]
        + [
            pltpu.VMEM((EH, N + 2 * H), BF),
            pltpu.VMEM((2, EH, H), BF),
            pltpu.VMEM((PROC, 1, 128), F32),
            pltpu.VMEM((DOM, 1, 128), F32),
            pltpu.VMEM((PROC, CAP, EH), BF),
            pltpu.VMEM((DOM, CAP, EH), BF),
            pltpu.VMEM((DOM, CAP, EH), BF),
            pltpu.VMEM((PROC, CAP, EH), BF),
            pltpu.VMEM((D, N), F32),
            pltpu.VMEM((N, D), F32),
            dma((len(args),)),
            dma((2,)),
            dma((2,)),
            dma(()),
            dma(()),
            dma(()),
            dma(()),
            dma(()),
            dma(()),
            dma((3,)),
        ],
        compiler_params=pltpu.CompilerParams(
            collective_id=0, has_side_effects=True, vmem_limit_bytes=60 * 1024 * 1024
        ),
    )(*args)


def solution(mesh):
    part = P(("grp", "dom"))
    return jax.shard_map(
        local,
        mesh=mesh,
        in_specs=(part,) + (P(),) * 10 + (part,) * 6,
        out_specs=part,
        check_vma=False,
    )
```

```python
import jax
import jax.numpy as jnp
from jax import lax
from jax.experimental import pallas as pl
from jax.experimental.pallas import tpu as pltpu
from jax.sharding import PartitionSpec as P

MESH = pl.DeviceIdType.MESH
BF = jnp.bfloat16
F32 = jnp.float32
I32 = jnp.int32

GRP = 8
DOM = 64
ZS = 16
YS = 4
N = 256
D = 512
EH = 256
H = 128
DEG = 8
ROWS = 64
RC = 32
RB = 128
SLOTS = 16
PZ = 4
PROC = YS * PZ
OWN = DOM // PROC
CAP = 2 * OWN
NODES_C = OWN * SLOTS


def iota(shape, dim):
    return lax.broadcasted_iota(I32, shape, dim)


def dot(a, b):
    return jnp.dot(a, b, preferred_element_type=F32)


def silu(v):
    return v * (0.5 + 0.5 * jnp.tanh(0.5 * v))


def kernel(*refs):
    ins, (out,), scratch = refs[:17], refs[17:18], refs[18:]
    bufs, rest = scratch[:17], scratch[17:]
    (
        nodes,
        w_cin,
        own,
        slot,
        ids,
        w_send,
        halo_ids,
        w_recv,
        edge_bias,
        w_msg,
        nbr,
        mask,
        w_self,
        gain,
        w_agg,
        coarse_bias,
        w_cout,
    ) = bufs
    (
        table,
        halo_out,
        send_ids,
        recv_ids,
        send_buf,
        recv_buf,
        back_buf,
        ret_buf,
        agg,
        base,
        load_sem,
        halo_ssem,
        halo_rsem,
        i_ssem,
        i_rsem,
        c_ssem,
        c_rsem,
        r_ssem,
        r_rsem,
        own_sem,
    ) = rest
    g = lax.axis_index("grp")
    me = lax.axis_index("dom")
    my_y, my_z = me // ZS, lax.rem(me, ZS)
    lower = lax.rem(g + GRP - 1, GRP)
    upper = lax.rem(g + 1, GRP)
    is_proc = my_z < PZ
    my_proc = jnp.where(is_proc, my_z * YS + my_y, 0)

    def proc_device(j):
        return lax.rem(j, YS) * ZS + j // YS

    loads = [pltpu.make_async_copy(ins[i], bufs[i], load_sem.at[i]) for i in range(17)]
    for i in (2, 3, 4, 0, 1):
        loads[i].start()

    barrier = pltpu.get_barrier_semaphore()
    for t in (lower, upper):
        pl.semaphore_signal(barrier, inc=1, device_id=(t, me), device_id_type=MESH)

    def by_z(k):
        return lax.rem(my_y + k, YS) * ZS + k // YS

    @pl.when(is_proc)
    def _():
        def greet(k, carry):
            t = by_z(k)

            @pl.when(t != me)
            def _():
                pl.semaphore_signal(barrier, inc=1, device_id=(g, t), device_id_type=MESH)

            return carry

        lax.fori_loop(0, DOM, greet, 0)

    for i in range(5, 17):
        loads[i].start()

    for i in (2, 3, 4):
        loads[i].wait()
    own_row = own[...].astype(F32)
    eye = iota((ROWS, ROWS), 0) == iota((ROWS, ROWS), 1)
    own_col = jnp.sum(jnp.where(eye, own_row, 0.0), axis=1, keepdims=True)
    before = (own_col == own_row) & (iota((ROWS, ROWS), 0) < iota((ROWS, ROWS), 1))
    rank = jnp.sum(before.astype(F32), axis=0, keepdims=True).astype(I32)
    pos = own[...] * 2 + rank
    place = (iota((2 * DOM, ROWS), 0) == pos).astype(F32).astype(BF)
    value = (lax.rem(own[...], OWN) * SLOTS + slot[...] + 1).astype(F32)
    at_proc = (iota((PROC, ROWS), 0) == pos // CAP).astype(F32).astype(BF)
    at_lane = jnp.where(iota((128, ROWS), 0) == lax.rem(pos, CAP), value, 0.0).astype(BF)
    coarse_ids = (
        lax.dot_general(at_proc, at_lane, (((1,), (1,)), ((), ())), preferred_element_type=F32)
        - 1.0
    )
    send_ids[...] = coarse_ids.reshape(PROC, 1, 128)
    row_of = ids[...] + (iota((1, N), 1) // RB) * RC
    member = (iota((ROWS, N), 0) == row_of).astype(F32).astype(BF)
    spread = dot(place, member)
    collect = spread.astype(BF)

    def to_procs(src, dst, ssem, rsem):
        def body(k, carry):
            j = lax.rem(my_z * YS + my_y + k, PROC)
            t = proc_device(j)

            @pl.when(t != me)
            def _():
                pltpu.make_async_remote_copy(
                    src_ref=src.at[j],
                    dst_ref=dst.at[me],
                    send_sem=ssem,
                    recv_sem=rsem,
                    device_id=(g, t),
                    device_id_type=MESH,
                ).start()

            return carry

        lax.fori_loop(0, PROC, body, 0)

    def await_bytes(ref, count, sem):
        part = ref.at[pl.ds(0, count)]
        pltpu.make_async_copy(part, part, sem).wait()

    loads[0].wait()
    restricted = (dot(collect, nodes[...]) * 0.25).astype(BF)
    loads[1].wait()
    coarse_in = dot(restricted, w_cin[...]).astype(BF)
    send_buf[...] = coarse_in.reshape(PROC, CAP, EH)
    pl.semaphore_wait(barrier, jnp.where(is_proc, PROC - 1, PROC) + 2)
    to_procs(send_ids, recv_ids, i_ssem, i_rsem)
    to_procs(send_buf, recv_buf, c_ssem, c_rsem)

    loads[5].wait()
    loads[6].wait()
    proj = dot(nodes[...], w_send[...]).T.astype(BF)
    table[:, 0:N] = proj
    halos = []
    for i, t in ((0, lower), (1, upper)):
        pick = (iota((N, H), 0) == halo_ids[0, i : i + 1, :]).astype(F32).astype(BF)
        halo_out[i] = dot(proj, pick).astype(BF)
        c = pltpu.make_async_remote_copy(
            src_ref=halo_out.at[i],
            dst_ref=table.at[:, pl.ds(N + H * (1 - i), H)],
            send_sem=halo_ssem.at[i],
            recv_sem=halo_rsem.at[i],
            device_id=(t, me),
            device_id_type=MESH,
        )
        c.start()
        halos.append(c)

    loads[7].wait()
    loads[8].wait()
    recv = (dot(nodes[...], w_recv[...]) + edge_bias[...]).T
    for i in (9, 10, 11, 12, 13, 14, 15, 16):
        loads[i].wait()
    base[...] = dot(nodes[...], w_self[...])
    w_msg_t = w_msg[...].T
    agg[...] = jnp.zeros_like(agg)
    spread = spread.T.astype(BF)
    for c in halos:
        c.wait()

    for k in range(DEG):
        pick = (iota((N + 2 * H, N), 0) == nbr[k : k + 1, :]).astype(F32).astype(BF)
        hid = silu(dot(table[...], pick) + recv).astype(BF)
        msg = dot(w_msg_t, hid)
        mean = jnp.mean(msg, axis=0, keepdims=True)
        msg = msg - mean
        var = jnp.mean(msg * msg, axis=0, keepdims=True)
        scale = lax.rsqrt(var + 1e-05) * mask[k : k + 1, :].astype(F32)
        agg[...] += msg * scale
    aggregate = (agg[...].T * gain[...]).astype(BF)
    change = silu(base[...] + dot(aggregate, w_agg[...]))
    base[...] = nodes[...].astype(F32) + change

    @pl.when(is_proc)
    def _():
        own_ids = pltpu.make_async_copy(send_ids.at[my_proc], recv_ids.at[me], own_sem.at[0])
        own_rows = pltpu.make_async_copy(send_buf.at[my_proc], recv_buf.at[me], own_sem.at[1])
        own_ids.start()
        own_rows.start()
        own_ids.wait()
        await_bytes(recv_ids, DOM - 1, i_rsem)
        got_ids = recv_ids[...].reshape(DOM, 128).astype(BF)
        total = DOM * CAP
        from_dev = (iota((DOM, total), 0) == iota((DOM, total), 1) // CAP).astype(F32).astype(BF)
        by_lane = lax.dot_general(
            got_ids, from_dev, (((0,), (0,)), ((), ())), preferred_element_type=F32
        )[0:CAP]
        mine = iota((CAP, total), 0) == lax.rem(iota((CAP, total), 1), CAP)
        id_row = jnp.sum(jnp.where(mine, by_lane, 0.0), axis=0, keepdims=True)
        holds = (iota((NODES_C, total), 0).astype(F32) == id_row).astype(F32)
        holds_t = holds.T.astype(BF)
        holds = holds.astype(BF)
        own_rows.wait()
        await_bytes(recv_buf, DOM - 1, c_rsem)
        summed = dot(holds, recv_buf[...].reshape(total, EH))
        coarse_hid = silu(summed + coarse_bias[...]).astype(BF)
        back_buf[...] = dot(holds_t, coarse_hid).astype(BF).reshape(DOM, CAP, EH)

        def send_back(k, carry):
            t = by_z(k)

            @pl.when(t != me)
            def _():
                pltpu.make_async_remote_copy(
                    src_ref=back_buf.at[t],
                    dst_ref=ret_buf.at[my_proc],
                    send_sem=r_ssem,
                    recv_sem=r_rsem,
                    device_id=(g, t),
                    device_id_type=MESH,
                ).start()

            return carry

        lax.fori_loop(0, DOM, send_back, 0)
        own_back = pltpu.make_async_copy(back_buf.at[me], ret_buf.at[my_proc], own_sem.at[2])
        own_back.start()
        own_back.wait()
        await_bytes(send_ids, PROC - 1, i_ssem)
        await_bytes(send_buf, PROC - 1, c_ssem)
        await_bytes(ret_buf, PROC - 1, r_rsem)

    @pl.when(jnp.logical_not(is_proc))
    def _():
        await_bytes(send_ids, PROC, i_ssem)
        await_bytes(send_buf, PROC, c_ssem)
        await_bytes(ret_buf, PROC, r_rsem)

    coarse_out = dot(ret_buf[...].reshape(2 * DOM, EH), w_cout[...]).astype(BF)
    out[...] = (base[...] + dot(spread, coarse_out)).astype(BF)

    @pl.when(is_proc)
    def _():
        await_bytes(back_buf, DOM - 1, r_ssem)


def local(
    nodes,
    w_send,
    w_recv,
    edge_bias,
    w_msg,
    msg_gain,
    w_self,
    w_agg,
    w_coarse_in,
    coarse_bias,
    w_coarse_out,
    halo_send,
    neighbours,
    edge_mask,
    restrict_ids,
    coarse_holder_index,
    coarse_slot,
):
    hbm = pl.BlockSpec(memory_space=pltpu.HBM)
    dma = pltpu.SemaphoreType.DMA
    args = (
        nodes,
        w_coarse_in,
        coarse_holder_index.T,
        coarse_slot.T,
        restrict_ids.reshape(1, N),
        w_send,
        halo_send,
        w_recv,
        edge_bias.reshape(1, EH),
        w_msg,
        neighbours.T,
        edge_mask.T,
        w_self,
        msg_gain.reshape(1, D),
        w_agg,
        coarse_bias.reshape(1, EH),
        w_coarse_out,
    )
    return pl.pallas_call(
        kernel,
        out_shape=jax.ShapeDtypeStruct((N, D), BF),
        in_specs=[hbm] * len(args),
        out_specs=pl.BlockSpec(memory_space=pltpu.VMEM),
        scratch_shapes=[pltpu.VMEM(a.shape, a.dtype) for a in args]
        + [
            pltpu.VMEM((EH, N + 2 * H), BF),
            pltpu.VMEM((2, EH, H), BF),
            pltpu.VMEM((PROC, 1, 128), F32),
            pltpu.VMEM((DOM, 1, 128), F32),
            pltpu.VMEM((PROC, CAP, EH), BF),
            pltpu.VMEM((DOM, CAP, EH), BF),
            pltpu.VMEM((DOM, CAP, EH), BF),
            pltpu.VMEM((PROC, CAP, EH), BF),
            pltpu.VMEM((D, N), F32),
            pltpu.VMEM((N, D), F32),
            dma((len(args),)),
            dma((2,)),
            dma((2,)),
            dma(()),
            dma(()),
            dma(()),
            dma(()),
            dma(()),
            dma(()),
            dma((3,)),
        ],
        compiler_params=pltpu.CompilerParams(
            collective_id=0, has_side_effects=True, vmem_limit_bytes=32 * 1024 * 1024
        ),
    )(*(pltpu.with_memory_space_constraint(a, pltpu.HBM) for a in args))


def solution(mesh):
    part = P(("grp", "dom"))
    return jax.shard_map(
        local,
        mesh=mesh,
        in_specs=(part,) + (P(),) * 10 + (part,) * 6,
        out_specs=part,
        check_vma=False,
    )
```

```python
import jax
import jax.numpy as jnp
from jax import lax
from jax.experimental import pallas as pl
from jax.experimental.pallas import tpu as pltpu
from jax.sharding import PartitionSpec as P

MESH = pl.DeviceIdType.MESH
BF = jnp.bfloat16
F32 = jnp.float32
I32 = jnp.int32

GRP = 8
DOM = 64
ZS = 16
YS = 4
N = 256
D = 512
EH = 256
H = 128
DEG = 8
ROWS = 64
RC = 32
RB = 128
SLOTS = 16
PZ = 4
PROC = YS * PZ
OWN = DOM // PROC
CAP = 2 * OWN
NODES_C = OWN * SLOTS


def iota(shape, dim):
    return lax.broadcasted_iota(I32, shape, dim)


def dot(a, b):
    return jnp.dot(a, b, preferred_element_type=F32)


def silu(v):
    return v * (0.5 + 0.5 * jnp.tanh(0.5 * v))


def kernel(*refs):
    ins, (out,), scratch = refs[:17], refs[17:18], refs[18:]
    bufs, rest = scratch[:17], scratch[17:]
    (
        nodes,
        w_cin,
        own,
        slot,
        ids,
        w_send,
        halo_ids,
        w_recv,
        edge_bias,
        w_msg,
        nbr,
        mask,
        w_self,
        gain,
        w_agg,
        coarse_bias,
        w_cout,
    ) = bufs
    (
        table,
        halo_out,
        send_ids,
        recv_ids,
        send_buf,
        recv_buf,
        back_buf,
        ret_buf,
        agg,
        base,
        load_sem,
        halo_ssem,
        halo_rsem,
        i_ssem,
        i_rsem,
        c_ssem,
        c_rsem,
        r_ssem,
        r_rsem,
        own_sem,
    ) = rest
    g = lax.axis_index("grp")
    me = lax.axis_index("dom")
    my_y, my_z = me // ZS, lax.rem(me, ZS)
    lower = lax.rem(g + GRP - 1, GRP)
    upper = lax.rem(g + 1, GRP)
    is_proc = my_z < PZ
    my_proc = jnp.where(is_proc, my_z * YS + my_y, 0)

    def proc_device(j):
        return lax.rem(j, YS) * ZS + j // YS

    loads = [pltpu.make_async_copy(ins[i], bufs[i], load_sem.at[i]) for i in range(17)]
    for i in (2, 3, 4, 0, 1):
        loads[i].start()

    barrier = pltpu.get_barrier_semaphore()
    for t in (lower, upper):
        pl.semaphore_signal(barrier, inc=1, device_id=(t, me), device_id_type=MESH)

    def by_z(k):
        return lax.rem(my_y + k, YS) * ZS + k // YS

    @pl.when(is_proc)
    def _():
        def greet(k, carry):
            t = by_z(k)

            @pl.when(t != me)
            def _():
                pl.semaphore_signal(barrier, inc=1, device_id=(g, t), device_id_type=MESH)

            return carry

        lax.fori_loop(0, DOM, greet, 0)

    for i in range(5, 17):
        loads[i].start()

    for i in (2, 3, 4):
        loads[i].wait()
    own_row = own[...].astype(F32)
    eye = iota((ROWS, ROWS), 0) == iota((ROWS, ROWS), 1)
    own_col = jnp.sum(jnp.where(eye, own_row, 0.0), axis=1, keepdims=True)
    before = (own_col == own_row) & (iota((ROWS, ROWS), 0) < iota((ROWS, ROWS), 1))
    rank = jnp.sum(before.astype(F32), axis=0, keepdims=True).astype(I32)
    pos = own[...] * 2 + rank
    place = (iota((2 * DOM, ROWS), 0) == pos).astype(F32).astype(BF)
    value = (lax.rem(own[...], OWN) * SLOTS + slot[...] + 1).astype(F32)
    at_proc = (iota((PROC, ROWS), 0) == pos // CAP).astype(F32).astype(BF)
    at_lane = jnp.where(iota((128, ROWS), 0) == lax.rem(pos, CAP), value, 0.0).astype(BF)
    coarse_ids = (
        lax.dot_general(at_proc, at_lane, (((1,), (1,)), ((), ())), preferred_element_type=F32)
        - 1.0
    )
    send_ids[...] = coarse_ids.reshape(PROC, 1, 128)
    row_of = ids[...] + (iota((1, N), 1) // RB) * RC
    member = (iota((ROWS, N), 0) == row_of).astype(F32).astype(BF)
    spread = dot(place, member)
    collect = spread.astype(BF)

    def to_procs(src, dst, ssem, rsem):
        def body(k, carry):
            j = k // YS * YS + lax.rem(my_y + k, YS)
            t = proc_device(j)

            @pl.when(t != me)
            def _():
                pltpu.make_async_remote_copy(
                    src_ref=src.at[j],
                    dst_ref=dst.at[me],
                    send_sem=ssem,
                    recv_sem=rsem,
                    device_id=(g, t),
                    device_id_type=MESH,
                ).start()

            return carry

        lax.fori_loop(0, PROC, body, 0)

    def await_bytes(ref, count, sem):
        part = ref.at[pl.ds(0, count)]
        pltpu.make_async_copy(part, part, sem).wait()

    loads[0].wait()
    restricted = (dot(collect, nodes[...]) * 0.25).astype(BF)
    loads[1].wait()
    coarse_in = dot(restricted, w_cin[...]).astype(BF)
    send_buf[...] = coarse_in.reshape(PROC, CAP, EH)
    pl.semaphore_wait(barrier, jnp.where(is_proc, PROC - 1, PROC) + 2)
    to_procs(send_ids, recv_ids, i_ssem, i_rsem)
    to_procs(send_buf, recv_buf, c_ssem, c_rsem)

    loads[5].wait()
    loads[6].wait()
    proj = dot(nodes[...], w_send[...]).T.astype(BF)
    table[:, 0:N] = proj
    halos = []
    for i, t in ((0, lower), (1, upper)):
        pick = (iota((N, H), 0) == halo_ids[0, i : i + 1, :]).astype(F32).astype(BF)
        halo_out[i] = dot(proj, pick).astype(BF)
        c = pltpu.make_async_remote_copy(
            src_ref=halo_out.at[i],
            dst_ref=table.at[:, pl.ds(N + H * (1 - i), H)],
            send_sem=halo_ssem.at[i],
            recv_sem=halo_rsem.at[i],
            device_id=(t, me),
            device_id_type=MESH,
        )
        c.start()
        halos.append(c)

    loads[7].wait()
    loads[8].wait()
    recv = (dot(nodes[...], w_recv[...]) + edge_bias[...]).T
    for i in (9, 10, 11, 12, 13, 14, 15, 16):
        loads[i].wait()
    base[...] = dot(nodes[...], w_self[...])
    w_msg_t = w_msg[...].T
    agg[...] = jnp.zeros_like(agg)
    spread = spread.T.astype(BF)
    for c in halos:
        c.wait()

    for k in range(DEG):
        pick = (iota((N + 2 * H, N), 0) == nbr[k : k + 1, :]).astype(F32).astype(BF)
        hid = silu(dot(table[...], pick) + recv).astype(BF)
        msg = dot(w_msg_t, hid)
        mean = jnp.mean(msg, axis=0, keepdims=True)
        msg = msg - mean
        var = jnp.mean(msg * msg, axis=0, keepdims=True)
        scale = lax.rsqrt(var + 1e-05) * mask[k : k + 1, :].astype(F32)
        agg[...] += msg * scale
    aggregate = (agg[...].T * gain[...]).astype(BF)
    change = silu(base[...] + dot(aggregate, w_agg[...]))
    base[...] = nodes[...].astype(F32) + change

    @pl.when(is_proc)
    def _():
        own_ids = pltpu.make_async_copy(send_ids.at[my_proc], recv_ids.at[me], own_sem.at[0])
        own_rows = pltpu.make_async_copy(send_buf.at[my_proc], recv_buf.at[me], own_sem.at[1])
        own_ids.start()
        own_rows.start()
        own_ids.wait()
        await_bytes(recv_ids, DOM - 1, i_rsem)
        got_ids = recv_ids[...].reshape(DOM, 128).astype(BF)
        total = DOM * CAP
        from_dev = (iota((DOM, total), 0) == iota((DOM, total), 1) // CAP).astype(F32).astype(BF)
        by_lane = lax.dot_general(
            got_ids, from_dev, (((0,), (0,)), ((), ())), preferred_element_type=F32
        )[0:CAP]
        mine = iota((CAP, total), 0) == lax.rem(iota((CAP, total), 1), CAP)
        id_row = jnp.sum(jnp.where(mine, by_lane, 0.0), axis=0, keepdims=True)
        holds = (iota((NODES_C, total), 0).astype(F32) == id_row).astype(F32)
        holds_t = holds.T.astype(BF)
        holds = holds.astype(BF)
        own_rows.wait()
        await_bytes(recv_buf, DOM - 1, c_rsem)
        summed = dot(holds, recv_buf[...].reshape(total, EH))
        coarse_hid = silu(summed + coarse_bias[...]).astype(BF)
        back_buf[...] = dot(holds_t, coarse_hid).astype(BF).reshape(DOM, CAP, EH)

        def send_back(k, carry):
            t = by_z(k)

            @pl.when(t != me)
            def _():
                pltpu.make_async_remote_copy(
                    src_ref=back_buf.at[t],
                    dst_ref=ret_buf.at[my_proc],
                    send_sem=r_ssem,
                    recv_sem=r_rsem,
                    device_id=(g, t),
                    device_id_type=MESH,
                ).start()

            return carry

        lax.fori_loop(0, DOM, send_back, 0)
        own_back = pltpu.make_async_copy(back_buf.at[me], ret_buf.at[my_proc], own_sem.at[2])
        own_back.start()
        own_back.wait()
        await_bytes(send_ids, PROC - 1, i_ssem)
        await_bytes(send_buf, PROC - 1, c_ssem)
        await_bytes(ret_buf, PROC - 1, r_rsem)

    @pl.when(jnp.logical_not(is_proc))
    def _():
        await_bytes(send_ids, PROC, i_ssem)
        await_bytes(send_buf, PROC, c_ssem)
        await_bytes(ret_buf, PROC, r_rsem)

    coarse_out = dot(ret_buf[...].reshape(2 * DOM, EH), w_cout[...]).astype(BF)
    out[...] = (base[...] + dot(spread, coarse_out)).astype(BF)

    @pl.when(is_proc)
    def _():
        await_bytes(back_buf, DOM - 1, r_ssem)


def local(
    nodes,
    w_send,
    w_recv,
    edge_bias,
    w_msg,
    msg_gain,
    w_self,
    w_agg,
    w_coarse_in,
    coarse_bias,
    w_coarse_out,
    halo_send,
    neighbours,
    edge_mask,
    restrict_ids,
    coarse_holder_index,
    coarse_slot,
):
    hbm = pl.BlockSpec(memory_space=pltpu.HBM)
    dma = pltpu.SemaphoreType.DMA
    args = (
        nodes,
        w_coarse_in,
        coarse_holder_index.T,
        coarse_slot.T,
        restrict_ids.reshape(1, N),
        w_send,
        halo_send,
        w_recv,
        edge_bias.reshape(1, EH),
        w_msg,
        neighbours.T,
        edge_mask.T,
        w_self,
        msg_gain.reshape(1, D),
        w_agg,
        coarse_bias.reshape(1, EH),
        w_coarse_out,
    )
    return pl.pallas_call(
        kernel,
        out_shape=jax.ShapeDtypeStruct((N, D), BF),
        in_specs=[hbm] * len(args),
        out_specs=pl.BlockSpec(memory_space=pltpu.VMEM),
        scratch_shapes=[pltpu.VMEM(a.shape, a.dtype) for a in args]
        + [
            pltpu.VMEM((EH, N + 2 * H), BF),
            pltpu.VMEM((2, EH, H), BF),
            pltpu.VMEM((PROC, 1, 128), F32),
            pltpu.VMEM((DOM, 1, 128), F32),
            pltpu.VMEM((PROC, CAP, EH), BF),
            pltpu.VMEM((DOM, CAP, EH), BF),
            pltpu.VMEM((DOM, CAP, EH), BF),
            pltpu.VMEM((PROC, CAP, EH), BF),
            pltpu.VMEM((D, N), F32),
            pltpu.VMEM((N, D), F32),
            dma((len(args),)),
            dma((2,)),
            dma((2,)),
            dma(()),
            dma(()),
            dma(()),
            dma(()),
            dma(()),
            dma(()),
            dma((3,)),
        ],
        compiler_params=pltpu.CompilerParams(
            collective_id=0, has_side_effects=True, vmem_limit_bytes=32 * 1024 * 1024
        ),
    )(*(pltpu.with_memory_space_constraint(a, pltpu.HBM) for a in args))


def solution(mesh):
    part = P(("grp", "dom"))
    return jax.shard_map(
        local,
        mesh=mesh,
        in_specs=(part,) + (P(),) * 10 + (part,) * 6,
        out_specs=part,
        check_vma=False,
    )
```
